256 devices in a mesh: blk: 64 (over y_lo, x, z), uly: 4 (over y_hi, core).
Axes of the slice: x: 4, y: 4 (y_hi: 2, y_lo: 2; y = y_hi * 2 + y_lo), z: 8, core: 2. Of those that a mesh axis runs over, the one named last changes fastest.
Arguments:
- queries: bfloat16 [32768, 3072], P(('blk', 'uly')), may hold values from -40 to 40
- keys: bfloat16 [32768, 3072], P(('blk', 'uly')), may hold values from -8 to 8
- values: bfloat16 [32768, 3072], P(('blk', 'uly')), may hold values from -6 to 6
- tile_order: int32 [256], replicated, may hold values from 0 to 255, as said below
- tile_mask: int32 [256, 20], replicated, may hold values from 0 to 1, as said below
Outputs:
- attended: bfloat16 [32768, 3072], P(('blk', 'uly'))
The draws below stay inside these ranges and needn't reach their ends.
Inputs may be any that keep to these rules, and one draw needn't show every extreme that they name: `tile_order`: entries 4 * f to 4 * f + 3 are a permutation of the tile numbers 4 * f to 4 * f + 3: every slot holds a tile of its own frame. tile_mask[a, (e + 2) * 4 + b] is 1 where tile a may attend to tile 4 * (a // 4 + e) + b; it is 0 where a // 4 + e is not a frame; tile_mask[a, 8 + a % 4] is 1.
All inputs are finite; a program needn't handle non-finite values.
Results may differ from the reference program's by a relative error of at most 0.0055.
Values may be sent and summed in bfloat16 or wider, within the bound.
No kernel may reach another device: no remote copies, remote signals or barrier semaphores. Data moves between devices by JAX's collectives and lax.ppermute only.
A program may use at most 64 MiB of HBM per device.

```python
import math
import jax
import jax.numpy as jnp
from jax import lax

D = 3072
HEADS = 24
HEAD = 128
TOK_DEV = 128
TPS = 4
REACH = 2
FRAMES = 64
TILES = 256
WIN = 20
TOKENS = 32768
N_ULY = 4


def draw_pair(key):
    base_key = jax.random.fold_in(key, 1701)
    key_draw, query_draw = jax.random.split(base_key, 2)
    keys_out = jnp.clip(jax.random.normal(key_draw, (TOKENS, D), jnp.float32), -6.0, 6.0)
    query_out = 2.5 * jnp.clip(jax.random.normal(query_draw, (TOKENS, D), jnp.float32), -6.0, 6.0)
    return (query_out, keys_out)


def draw_queries(key, part):
    return draw_pair(key)[0].astype(jnp.bfloat16)


def draw_keys(key, part):
    return draw_pair(key)[1].astype(jnp.bfloat16)


def draw_tile_order(key, part):
    frame_keys = jax.random.split(jax.random.fold_in(key, 23), FRAMES)
    within = jax.vmap(lambda frame_key: jax.random.permutation(frame_key, TPS))(frame_keys)
    shifted = within.astype(jnp.int32) + jnp.arange(FRAMES, dtype=jnp.int32)[:, None] * TPS
    return shifted.reshape(TILES).astype(jnp.int32)


def draw_tile_mask(key, part):
    tile_ids = jnp.arange(TILES, dtype=jnp.int32)[:, None]
    column_ids = jnp.arange(WIN, dtype=jnp.int32)[None, :]
    frame_of = tile_ids // TPS
    spatial = tile_ids % TPS
    offset = column_ids // TPS - REACH
    other = column_ids % TPS
    inside = (frame_of + offset >= 0) & (frame_of + offset < FRAMES)
    half_width = TPS // 2
    near = jnp.abs(spatial % half_width - other % half_width) <= 1
    keep = jax.random.randint(jax.random.fold_in(key, 41), (TILES, WIN), 0, 4) > 0
    own_tile = (offset == 0) & (other == spatial)
    return jnp.where(own_tile | inside & near & keep, 1, 0).astype(jnp.int32)


def levels(rng, shape, cuts, low, top_value):
    def one(axis_at, parts):
        draws = jax.random.uniform(jax.random.fold_in(jax.random.fold_in(rng, 6), axis_at), (parts,), jnp.float32, low / len(cuts), top_value / len(cuts))
        return jnp.repeat(jnp.exp(draws), shape[axis_at] // parts).reshape((-1,) + (1,) * (len(shape) - axis_at - 1))

    factor_of = one(*cuts[0])
    for cut in cuts[1:]:
        factor_of = factor_of * one(*cut)
    return factor_of


def gaussian(key, shape, deviation, most, shards=(), kind=jnp.bfloat16):
    level = levels(key, shape, shards, -0.22, 0.18) if shards else 1.0
    entries = jax.random.normal(key, shape, jnp.float32) * deviation * level
    return jnp.minimum(jnp.maximum(entries, -most), most).astype(kind)


def setup_inputs(seed: int = 0) -> dict:
    streams_of = jax.random.split(jax.random.key(seed), 6)
    queries = draw_queries(jax.random.fold_in(streams_of[5], 71), 0)
    keys = draw_keys(jax.random.fold_in(streams_of[5], 71), 0)
    values = gaussian(streams_of[2], (TOKENS, D), 1.0, 6.0, ((0, 256),))
    tile_order = draw_tile_order(jax.random.fold_in(streams_of[5], 71), 0)
    tile_mask = draw_tile_mask(jax.random.fold_in(streams_of[5], 71), 0)
    return {"queries": queries, "keys": keys, "values": values, "tile_order": tile_order, "tile_mask": tile_mask}


def select_matrix(indices, count):
    return (indices[:, None] == jnp.arange(count, dtype=jnp.int32)[None, :]).astype(jnp.float32)

def reference(queries, keys, values, tile_order, tile_mask):
    block_rows = TOK_DEV * N_ULY
    tile_rows = block_rows // TPS
    span_frames = 2 * REACH + 1
    scale = 1.0 / math.sqrt(HEAD)
    query_frames = queries.reshape(FRAMES, block_rows, HEADS, HEAD)
    blank = jnp.zeros((REACH, block_rows, HEADS, HEAD), jnp.bfloat16)
    key_frames = jnp.concatenate([blank, keys.reshape(FRAMES, block_rows, HEADS, HEAD), blank], axis=0)
    value_frames = jnp.concatenate([blank, values.reshape(FRAMES, block_rows, HEADS, HEAD), blank], axis=0)
    frame_ids = jnp.arange(FRAMES, dtype=jnp.int32)
    spatial = (tile_order.reshape(FRAMES, TPS) - frame_ids[:, None] * TPS).astype(jnp.int32)
    blank_order = jnp.zeros((REACH, TPS), jnp.int32)
    spatial_padded = jnp.concatenate([blank_order, spatial, blank_order], axis=0)
    mask_frames = tile_mask.reshape(FRAMES, TPS, WIN).astype(jnp.float32)

    def one_frame(frame_id):
        slot_rows = jnp.dot(select_matrix(spatial[frame_id], TPS), mask_frames[frame_id], precision=lax.Precision.HIGHEST, preferred_element_type=jnp.float32)
        pieces = []
        for offset in range(-REACH, REACH + 1):
            other_frame = frame_id + offset
            inside = ((other_frame >= 0) & (other_frame < FRAMES)).astype(jnp.float32)
            other_order = spatial_padded[other_frame + REACH]
            columns = slot_rows[:, (offset + REACH) * TPS:(offset + REACH + 1) * TPS]
            pieces.append(jnp.dot(columns, select_matrix(other_order, TPS).T, precision=lax.Precision.HIGHEST, preferred_element_type=jnp.float32) * inside)
        tile_allowed = jnp.concatenate(pieces, axis=1) > 0.5
        allowed = jnp.repeat(jnp.repeat(tile_allowed, tile_rows, axis=0), tile_rows, axis=1)
        local_keys = lax.dynamic_slice_in_dim(key_frames, frame_id, span_frames, 0)
        local_keys = local_keys.reshape(span_frames * block_rows, HEADS, HEAD)
        local_values = lax.dynamic_slice_in_dim(value_frames, frame_id, span_frames, 0)
        local_values = local_values.reshape(span_frames * block_rows, HEADS, HEAD)

        def one_head(operands):
            head_query, head_key, head_value = operands
            scores = jnp.dot(head_query, head_key.T, preferred_element_type=jnp.float32) * scale
            masked = jnp.where(allowed, scores, -1e+30)
            top_score = lax.optimization_barrier(jnp.max(masked, axis=1, keepdims=True))
            weights = jnp.where(allowed, jnp.exp(masked - top_score), 0.0)
            total = lax.optimization_barrier(jnp.sum(weights, axis=1, keepdims=True))
            summed = jnp.dot(weights.astype(jnp.bfloat16), head_value, preferred_element_type=jnp.float32)
            return (summed / total).astype(jnp.bfloat16)
        outputs = lax.map(one_head, (query_frames[frame_id].transpose(1, 0, 2), local_keys.transpose(1, 0, 2), local_values.transpose(1, 0, 2)))
        return outputs.transpose(1, 0, 2).reshape(block_rows, HEADS * HEAD)
    return lax.map(one_frame, frame_ids).reshape(TOKENS, D)
```

```python
import functools
import math

import jax
import jax.numpy as jnp
from jax import lax
from jax.experimental import pallas as pl
from jax.experimental.pallas import tpu as pltpu
from jax.sharding import PartitionSpec as P

HEAD = 128
TPS = 4
REACH = 2
SPAN = 2 * REACH + 1
CHUNKS = (2, 2, 2)
NEG = -1e30


def pack_kernel(groups, q_ref, k_ref, v_ref, *out_refs):
    width = q_ref.shape[1] // groups
    count = len(out_refs) // 2
    for u in range(groups):
        first = 0
        for c in range(count):
            kv_ref, qc_ref = out_refs[c], out_refs[count + c]
            cols = kv_ref.shape[-1]
            at = slice(u * width + first, u * width + first + cols)
            kv_ref[u, 0] = k_ref[:, at]
            kv_ref[u, 1] = v_ref[:, at]
            qc_ref[u] = q_ref[:, at]
            first += cols


def pack(queries, keys, values, groups, chunks):
    rows = queries.shape[0]
    kv = [jax.ShapeDtypeStruct((groups, 2, rows, n * HEAD), jnp.bfloat16) for n in chunks]
    q = [jax.ShapeDtypeStruct((groups, rows, n * HEAD), jnp.bfloat16) for n in chunks]
    outs = pl.pallas_call(
        functools.partial(pack_kernel, groups),
        out_shape=kv + q,
        name="pack",
    )(queries, keys, values)
    return outs[: len(chunks)], outs[len(chunks) :]


def unpack_kernel(groups, *refs):
    out_ref = refs[-1]
    width = out_ref.shape[1] // groups
    for u in range(groups):
        first = 0
        for ref in refs[:-1]:
            cols = ref.shape[-1]
            out_ref[:, u * width + first : u * width + first + cols] = ref[u]
            first += cols


def unpack(parts):
    groups, rows = parts[0].shape[:2]
    width = groups * sum(p.shape[-1] for p in parts)
    return pl.pallas_call(
        functools.partial(unpack_kernel, groups),
        out_shape=jax.ShapeDtypeStruct((rows, width), jnp.bfloat16),
        name="unpack",
    )(*parts)


def attend_kernel(scale, bias_ref, q_ref, *refs):
    kv_refs, out_ref, s_ref = refs[:SPAN], refs[SPAN], refs[SPAN + 1]
    rows = q_ref.shape[1]
    frame_rows = TPS * rows
    q = q_ref[...].reshape(frame_rows, HEAD)
    tops = [None] * TPS
    for e in range(SPAN):
        k = kv_refs[e][:, 0].reshape(frame_rows, HEAD)
        s = lax.dot_general(q, k, (((1,), (1,)), ((), ())), preferred_element_type=jnp.float32)
        for a in range(TPS):
            for b in range(TPS):
                block = s[a * rows : (a + 1) * rows, b * rows : (b + 1) * rows]
                block = block * scale + bias_ref[a * SPAN * TPS + e * TPS + b]
                s_ref[a, e * TPS + b] = block
                tops[a] = block if tops[a] is None else jnp.maximum(tops[a], block)
    tops = [jnp.max(top, axis=1, keepdims=True) for top in tops]
    sums = [None] * TPS
    accum = None
    for e in range(SPAN):
        weights = []
        for a in range(TPS):
            row = []
            for b in range(TPS):
                w = jnp.exp2(s_ref[a, e * TPS + b] - tops[a])
                sums[a] = w if sums[a] is None else sums[a] + w
                row.append(w.astype(jnp.bfloat16))
            weights.append(jnp.concatenate(row, axis=1))
        v = kv_refs[e][:, 1].reshape(frame_rows, HEAD)
        part = jnp.dot(
            jnp.concatenate(weights, axis=0), v, preferred_element_type=jnp.float32
        )
        accum = part if accum is None else accum + part
    for a in range(TPS):
        total = jnp.sum(sums[a], axis=1, keepdims=True)
        out_ref[a] = (accum[a * rows : (a + 1) * rows] / total).astype(out_ref.dtype)


def attend(bias, q, kvs):
    groups, rows, cols = q.shape
    heads = cols // HEAD
    keys = SPAN * groups * rows
    q_spec = pl.BlockSpec((groups, rows, HEAD), lambda h: (0, 0, h))
    kv_spec = pl.BlockSpec((groups, 2, rows, HEAD), lambda h: (0, 0, 0, h))
    return pl.pallas_call(
        functools.partial(attend_kernel, math.log2(math.e) / math.sqrt(HEAD)),
        grid=(heads,),
        in_specs=[pl.BlockSpec(memory_space=pltpu.SMEM), q_spec] + [kv_spec] * SPAN,
        out_specs=q_spec,
        out_shape=jax.ShapeDtypeStruct((groups, rows, cols), jnp.bfloat16),
        scratch_shapes=[pltpu.VMEM((TPS, SPAN * TPS, rows, rows), jnp.float32)],
        compiler_params=pltpu.CompilerParams(vmem_limit_bytes=32 * 1024 * 1024),
        cost_estimate=pl.CostEstimate(
            flops=4 * heads * groups * rows * keys * HEAD,
            bytes_accessed=2 * cols * (2 * groups * rows + 2 * keys),
            transcendentals=heads * groups * rows * keys,
        ),
        name="attend",
    )(bias, q, *kvs)


def tile_bias(tile_order, tile_mask, position, frames):
    pad = REACH * TPS
    padded = jnp.pad(tile_order, (pad, pad))
    near = lax.dynamic_slice_in_dim(padded, position * TPS, SPAN * TPS).reshape(SPAN, TPS)
    near_frames = position + jnp.arange(-REACH, REACH + 1, dtype=jnp.int32)[:, None]
    inside = (near_frames >= 0) & (near_frames < frames)
    spatial = near - near_frames * TPS
    own = lax.dynamic_slice_in_dim(tile_order, position * TPS, TPS) - position * TPS
    rows = lax.dynamic_slice_in_dim(tile_mask, position * TPS, TPS, 0).reshape(TPS, SPAN, TPS)
    ids = jnp.arange(TPS, dtype=jnp.int32)
    pick_q = own[:, None] == ids
    pick_k = (spatial[:, :, None] == ids) & inside[:, :, None]
    hit = (
        pick_q[:, None, None, :, None]
        & pick_k[None, :, :, None, :]
        & (rows != 0).transpose(1, 0, 2)[None, :, None, :, :]
    )
    allowed = jnp.any(hit, axis=(3, 4))
    return jnp.where(allowed, 0.0, NEG).astype(jnp.float32).reshape(-1)


def shifted(block, distance, frames):
    route = [(i, i + distance) for i in range(frames) if 0 <= i + distance < frames]
    return lax.ppermute(block, "blk", route)


def per_device(queries, keys, values, tile_order, tile_mask):
    groups = lax.axis_size("uly")
    frames = lax.axis_size("blk")
    position = lax.axis_index("blk")
    kv_parts, q_parts = pack(queries, keys, values, groups, CHUNKS)
    bias = tile_bias(tile_order, tile_mask, position, frames)
    outs = []
    for kv, q in zip(kv_parts, q_parts):
        own = lax.all_to_all(kv, "uly", split_axis=0, concat_axis=0, tiled=True)
        own_q = lax.all_to_all(q, "uly", split_axis=0, concat_axis=0, tiled=True)
        below = shifted(own, 1, frames)
        above = shifted(own, -1, frames)
        below2 = shifted(below, 1, frames)
        above2 = shifted(above, -1, frames)
        out = attend(bias, own_q, [below2, below, own, above, above2])
        outs.append(lax.all_to_all(out, "uly", split_axis=0, concat_axis=0, tiled=True))
    return unpack(outs)


def solution(mesh):
    return jax.shard_map(
        per_device,
        mesh=mesh,
        in_specs=(
            P(("blk", "uly"), None),
            P(("blk", "uly"), None),
            P(("blk", "uly"), None),
            P(),
            P(),
        ),
        out_specs=P(("blk", "uly"), None),
        check_vma=False,
    )
```

```python
import functools
import math

import jax
import jax.numpy as jnp
from jax import lax
from jax.experimental import pallas as pl
from jax.experimental.pallas import tpu as pltpu
from jax.sharding import PartitionSpec as P

HEAD = 128
TPS = 4
REACH = 2
SPAN = 2 * REACH + 1
CHUNKS = (3, 3)
NEG = -1e30
AXES = ("blk", "uly")


def member(u, far):
    return u if u % 2 == 0 else jnp.where(far, u ^ 2, u)


def copy_kernel(plan, groups, far_ref, *refs):
    far = far_ref[0] != 0
    for source, target, slot, first in plan:
        src, dst = refs[source], refs[target]
        width = src.shape[1] // groups
        cols = dst.shape[-1]
        for u in range(groups):
            start = pl.multiple_of(member(u, far) * width + first, HEAD)
            block = src[:, pl.ds(start, cols)]
            if slot is None:
                dst[u] = block
            else:
                dst[u, slot] = block


def pack_kv(keys, values, far, groups, chunks, skip):
    rows = keys.shape[0]
    plan, first = [], skip
    for c, n in enumerate(chunks):
        plan += [(0, 2 + c, 0, first * HEAD), (1, 2 + c, 1, first * HEAD)]
        first += n
    return pl.pallas_call(
        functools.partial(copy_kernel, plan, groups),
        in_specs=[pl.BlockSpec(memory_space=pltpu.SMEM)] + [pl.BlockSpec()] * 2,
        out_shape=[
            jax.ShapeDtypeStruct((groups, 2, rows, n * HEAD), jnp.bfloat16) for n in chunks
        ],
        name="pack_kv",
    )(far, keys, values)


def pack_q(queries, far, groups, chunks):
    rows = queries.shape[0]
    plan, first = [], 0
    for c, n in enumerate(chunks):
        plan.append((0, 1 + c, None, first * HEAD))
        first += n
    return pl.pallas_call(
        functools.partial(copy_kernel, plan, groups),
        in_specs=[pl.BlockSpec(memory_space=pltpu.SMEM), pl.BlockSpec()],
        out_shape=[jax.ShapeDtypeStruct((groups, rows, n * HEAD), jnp.bfloat16) for n in chunks],
        name="pack_q",
    )(far, queries)


def unpack_kernel(groups, far_ref, *refs):
    far = far_ref[0] != 0
    out_ref = refs[-1]
    width = out_ref.shape[1] // groups
    for u in range(groups):
        first = 0
        for ref in refs[:-1]:
            cols = ref.shape[-1]
            start = pl.multiple_of(member(u, far) * width + first, HEAD)
            out_ref[:, pl.ds(start, cols)] = ref[u]
            first += cols


def unpack(parts, far):
    groups, rows = parts[0].shape[:2]
    width = groups * sum(p.shape[-1] for p in parts)
    return pl.pallas_call(
        functools.partial(unpack_kernel, groups),
        in_specs=[pl.BlockSpec(memory_space=pltpu.SMEM)] + [pl.BlockSpec()] * len(parts),
        out_shape=jax.ShapeDtypeStruct((rows, width), jnp.bfloat16),
        name="unpack",
    )(far, *parts)


def attend_kernel(scale, bias_ref, q_ref, *refs):
    kv_refs, out_ref, s_ref = refs[:SPAN], refs[SPAN], refs[SPAN + 1]
    rows = q_ref.shape[1]
    frame_rows = TPS * rows
    q = q_ref[...].reshape(frame_rows, HEAD)
    tops = [None] * TPS
    for e in range(SPAN):
        k = kv_refs[e][:, 0].reshape(frame_rows, HEAD)
        s = lax.dot_general(k, q, (((1,), (1,)), ((), ())), preferred_element_type=jnp.float32)
        for b in range(TPS):
            for a in range(TPS):
                block = s[b * rows : (b + 1) * rows, a * rows : (a + 1) * rows]
                block = block + bias_ref[a * SPAN * TPS + e * TPS + b]
                s_ref[e * TPS + b, :, a * rows : (a + 1) * rows] = block
                top = jnp.max(block, axis=0, keepdims=True)
                tops[a] = top if tops[a] is None else jnp.maximum(tops[a], top)
    top = jnp.concatenate(tops, axis=1) * scale
    total = jnp.zeros((1, frame_rows), jnp.float32)
    accum = None
    for e in range(SPAN):
        s = s_ref[e * TPS : (e + 1) * TPS].reshape(frame_rows, frame_rows)
        w = jnp.exp2(s * scale - top)
        total = total + jnp.sum(w, axis=0, keepdims=True)
        v = kv_refs[e][:, 1].reshape(frame_rows, HEAD)
        part = lax.dot_general(
            v, w.astype(jnp.bfloat16), (((0,), (0,)), ((), ())), preferred_element_type=jnp.float32
        )
        accum = part if accum is None else accum + part
    out = (accum / total).T
    out_ref[...] = out.reshape(TPS, rows, HEAD).astype(out_ref.dtype)


def attend(bias, q, kvs, first):
    groups, rows, cols = kvs[0].shape[0], kvs[0].shape[2], kvs[0].shape[3]
    heads = cols // HEAD
    keys = SPAN * groups * rows
    kv_spec = pl.BlockSpec((groups, 2, rows, HEAD), lambda h: (0, 0, 0, h))
    return pl.pallas_call(
        functools.partial(attend_kernel, math.log2(math.e) / math.sqrt(HEAD)),
        grid=(heads,),
        in_specs=[
            pl.BlockSpec(memory_space=pltpu.SMEM),
            pl.BlockSpec((groups, rows, HEAD), lambda h: (0, 0, h + first)),
        ]
        + [kv_spec] * SPAN,
        out_specs=pl.BlockSpec((groups, rows, HEAD), lambda h: (0, 0, h)),
        out_shape=jax.ShapeDtypeStruct((groups, rows, cols), jnp.bfloat16),
        scratch_shapes=[pltpu.VMEM((SPAN * TPS, rows, TPS * rows), jnp.float32)],
        compiler_params=pltpu.CompilerParams(vmem_limit_bytes=32 * 1024 * 1024),
        cost_estimate=pl.CostEstimate(
            flops=4 * heads * groups * rows * keys * HEAD,
            bytes_accessed=2 * cols * (2 * groups * rows + 2 * keys),
            transcendentals=heads * groups * rows * keys,
        ),
        name="attend",
    )(bias, q, *kvs)


def tile_bias(tile_order, tile_mask, position, frames):
    pad = REACH * TPS
    padded = jnp.pad(tile_order, (pad, pad))
    near = lax.dynamic_slice_in_dim(padded, position * TPS, SPAN * TPS).reshape(SPAN, TPS)
    near_frames = position + jnp.arange(-REACH, REACH + 1, dtype=jnp.int32)[:, None]
    inside = (near_frames >= 0) & (near_frames < frames)
    spatial = near - near_frames * TPS
    own = lax.dynamic_slice_in_dim(tile_order, position * TPS, TPS) - position * TPS
    rows = lax.dynamic_slice_in_dim(tile_mask, position * TPS, TPS, 0).reshape(TPS, SPAN, TPS)
    ids = jnp.arange(TPS, dtype=jnp.int32)
    pick_q = own[:, None] == ids
    pick_k = (spatial[:, :, None] == ids) & inside[:, :, None]
    hit = (
        pick_q[:, None, None, :, None]
        & pick_k[None, :, :, None, :]
        & (rows != 0).transpose(1, 0, 2)[None, :, None, :, :]
    )
    allowed = jnp.any(hit, axis=(3, 4))
    return jnp.where(allowed, 0.0, NEG).astype(jnp.float32).reshape(-1)


def shifted(block, distance, frames, groups):
    route = []
    for i in range(frames):
        j = i + distance
        if 0 <= j < frames:
            trade = (i < frames // 2) != (j < frames // 2)
            for u in range(groups):
                to = u ^ 2 if trade and u % 2 else u
                route.append((i * groups + u, j * groups + to))
    return lax.ppermute(block, AXES, route)


def after(x, *others):
    return lax.optimization_barrier((x, *others))[0]


def exchanged(x):
    return lax.all_to_all(x, "uly", split_axis=0, concat_axis=0, tiled=True)


def per_device(queries, keys, values, tile_order, tile_mask):
    groups = lax.axis_size("uly")
    frames = lax.axis_size("blk")
    position = lax.axis_index("blk")
    far = (position >= frames // 2).astype(jnp.int32).reshape(1)
    (kv0,) = pack_kv(keys, values, far, groups, CHUNKS[:1], 0)
    (kv1,) = pack_kv(keys, values, far, groups, CHUNKS[1:], CHUNKS[0])
    (q,) = pack_q(queries, far, groups, (sum(CHUNKS),))
    bias = tile_bias(tile_order, tile_mask, position, frames)
    move = functools.partial(shifted, frames=frames, groups=groups)

    own0 = exchanged(kv0)
    up0, down0 = move(own0, 1), move(own0, -1)
    own1 = exchanged(after(kv1, own0))
    own_q = exchanged(after(q, up0))
    up1, down1 = move(own1, 1), move(own1, -1)
    up0b, down0b = move(up0, 1), move(down0, -1)
    up1b, down1b = move(up1, 1), move(down1, -1)
    out0 = attend(bias, own_q, [up0b, up0, own0, down0, down0b], 0)
    res0 = exchanged(out0)
    out1 = attend(bias, own_q, [up1b, up1, own1, down1, down1b], CHUNKS[0])
    res1 = exchanged(out1)
    return unpack([res0, res1], far)


def solution(mesh):
    return jax.shard_map(
        per_device,
        mesh=mesh,
        in_specs=(
            P(AXES, None),
            P(AXES, None),
            P(AXES, None),
            P(),
            P(),
        ),
        out_specs=P(AXES, None),
        check_vma=False,
    )
```

```python
import functools
import math

import jax
import jax.numpy as jnp
from jax import lax
from jax.experimental import pallas as pl
from jax.experimental.pallas import tpu as pltpu
from jax.sharding import PartitionSpec as P

HEAD = 128
TPS = 4
REACH = 2
SPAN = 2 * REACH + 1
CHUNKS = (3, 3)
NEG = -1e30
AXES = ("blk", "uly")


def run_copies(pairs, sems):
    copies = [pltpu.make_async_copy(src, dst, sems.at[i]) for i, (src, dst) in enumerate(pairs)]
    for copy in copies:
        copy.start()
    for copy in copies:
        copy.wait()


def pack_kv_kernel(groups, skip, k_ref, v_ref, out_ref, sems):
    width, cols = k_ref.shape[1] // groups, out_ref.shape[-1]
    pairs = []
    for u in range(groups):
        at = pl.ds(u * width + skip * HEAD, cols)
        pairs += [(k_ref.at[:, at], out_ref.at[u, 0]), (v_ref.at[:, at], out_ref.at[u, 1])]
    run_copies(pairs, sems)


def pack_kv(keys, values, groups, heads, skip):
    rows = keys.shape[0]
    return pl.pallas_call(
        functools.partial(pack_kv_kernel, groups, skip),
        in_specs=[pl.BlockSpec(memory_space=pl.ANY)] * 2,
        out_shape=jax.ShapeDtypeStruct((groups, 2, rows, heads * HEAD), jnp.bfloat16),
        scratch_shapes=[pltpu.SemaphoreType.DMA((2 * groups,))],
        name="pack_kv",
    )(keys, values)


def pack_q_kernel(groups, q_ref, out_ref, sems):
    width = q_ref.shape[1] // groups
    run_copies(
        [(q_ref.at[:, pl.ds(u * width, width)], out_ref.at[u]) for u in range(groups)], sems
    )


def pack_q(queries, groups):
    rows, cols = queries.shape
    return pl.pallas_call(
        functools.partial(pack_q_kernel, groups),
        in_specs=[pl.BlockSpec(memory_space=pl.ANY)],
        out_shape=jax.ShapeDtypeStruct((groups, rows, cols // groups), jnp.bfloat16),
        scratch_shapes=[pltpu.SemaphoreType.DMA((groups,))],
        name="pack_q",
    )(queries)


def unpack_kernel(groups, place_ref, first_ref, *refs):
    rest, out_ref = refs[:groups], refs[groups]
    width, cols = out_ref.shape[1] // groups, first_ref.shape[-1]
    place = place_ref[0]
    for u in range(groups):
        out_ref[:, u * width : u * width + cols] = first_ref[u]
    for t in range(groups):
        start = pl.multiple_of((place ^ t) * width + cols, HEAD)
        out_ref[:, pl.ds(start, width - cols)] = rest[t][...]


def unpack(place, first, rest):
    groups, rows, cols = first.shape
    width = groups * (cols + rest[0].shape[-1])
    return pl.pallas_call(
        functools.partial(unpack_kernel, groups),
        in_specs=[pl.BlockSpec(memory_space=pltpu.SMEM)] + [pl.BlockSpec()] * (1 + groups),
        out_shape=jax.ShapeDtypeStruct((rows, width), jnp.bfloat16),
        name="unpack",
    )(place, first, *rest)


def attend_kernel(scale, offsets, carried, final, spread, bias_ref, place_ref, q_ref, *refs):
    count = len(offsets)
    kv_refs, refs = refs[:count], refs[count:]
    s_ref, o_ref, refs = refs[-2], refs[-1], refs[:-2]
    rows = q_ref.shape[1]
    frame_rows = TPS * rows
    q = q_ref[...].reshape(frame_rows, HEAD)
    tops = [None] * TPS
    for i, offset in enumerate(offsets):
        e = offset + REACH
        k = kv_refs[i][:, 0].reshape(frame_rows, HEAD)
        s = lax.dot_general(k, q, (((1,), (1,)), ((), ())), preferred_element_type=jnp.float32)
        for b in range(TPS):
            for a in range(TPS):
                block = s[b * rows : (b + 1) * rows, a * rows : (a + 1) * rows]
                block = block + bias_ref[a * SPAN * TPS + e * TPS + b]
                s_ref[i * TPS + b, :, a * rows : (a + 1) * rows] = block
                top = jnp.max(block, axis=0, keepdims=True)
                tops[a] = top if tops[a] is None else jnp.maximum(tops[a], top)
    top = jnp.concatenate(tops, axis=1) * scale
    if carried:
        accum_ref, stats_ref = refs[:2]
        refs = refs[2:]
        before = stats_ref[0, 0:1]
        top = jnp.maximum(top, before)
        factor = jnp.exp2(before - top)
        total = stats_ref[0, 1:2] * factor
        accum = accum_ref[0] * factor
    else:
        total = jnp.zeros((1, frame_rows), jnp.float32)
        accum = None
    for i in range(count):
        s = s_ref[i * TPS : (i + 1) * TPS].reshape(frame_rows, frame_rows)
        w = jnp.exp2(s * scale - top)
        total = total + jnp.sum(w, axis=0, keepdims=True)
        v = kv_refs[i][:, 1].reshape(frame_rows, HEAD)
        part = lax.dot_general(
            v, w.astype(jnp.bfloat16), (((0,), (0,)), ((), ())), preferred_element_type=jnp.float32
        )
        accum = part if accum is None else accum + part
    if final:
        out = (accum / total).T.reshape(TPS, rows, HEAD).astype(jnp.bfloat16)
        if spread:
            o_ref[...] = out
            for t in range(TPS):
                refs[t][...] = o_ref[place_ref[0] ^ t]
        else:
            refs[0][...] = out
    else:
        refs[0][0] = accum
        refs[1][0, 0:1] = top
        refs[1][0, 1:2] = total


def attend(bias, place, q, kvs, first, carry=None, final=True, spread=False):
    offsets = sorted(kvs)
    groups, _, rows, cols = kvs[offsets[0]].shape
    heads = cols // HEAD
    queries = groups * rows
    keys = len(offsets) * queries
    kv_spec = pl.BlockSpec((groups, 2, rows, HEAD), lambda h: (0, 0, 0, h))
    state_specs = [
        pl.BlockSpec((1, HEAD, queries), lambda h: (h, 0, 0)),
        pl.BlockSpec((1, 2, queries), lambda h: (h, 0, 0)),
    ]
    if spread:
        out_specs = [pl.BlockSpec((rows, HEAD), lambda h: (0, h))] * groups
        out_shape = [jax.ShapeDtypeStruct((rows, cols), jnp.bfloat16)] * groups
    elif final:
        out_specs = pl.BlockSpec((groups, rows, HEAD), lambda h: (0, 0, h))
        out_shape = jax.ShapeDtypeStruct((groups, rows, cols), jnp.bfloat16)
    else:
        out_specs = state_specs
        out_shape = [
            jax.ShapeDtypeStruct((heads, HEAD, queries), jnp.float32),
            jax.ShapeDtypeStruct((heads, 2, queries), jnp.float32),
        ]
    return pl.pallas_call(
        functools.partial(
            attend_kernel,
            math.log2(math.e) / math.sqrt(HEAD),
            offsets,
            carry is not None,
            final,
            spread,
        ),
        grid=(heads,),
        in_specs=[
            pl.BlockSpec(memory_space=pltpu.SMEM),
            pl.BlockSpec(memory_space=pltpu.SMEM),
            pl.BlockSpec((groups, rows, HEAD), lambda h: (0, 0, h + first)),
        ]
        + [kv_spec] * len(offsets)
        + (state_specs if carry is not None else []),
        out_specs=out_specs,
        out_shape=out_shape,
        scratch_shapes=[
            pltpu.VMEM((len(offsets) * TPS, rows, queries), jnp.float32),
            pltpu.VMEM((TPS, rows, HEAD), jnp.bfloat16),
        ],
        compiler_params=pltpu.CompilerParams(vmem_limit_bytes=32 * 1024 * 1024),
        cost_estimate=pl.CostEstimate(
            flops=4 * heads * queries * keys * HEAD,
            bytes_accessed=2 * cols * (2 * queries + 2 * keys),
            transcendentals=heads * queries * keys,
        ),
        name="attend",
    )(bias, place, q, *[kvs[o] for o in offsets], *(carry or ()))


def tile_bias(tile_order, tile_mask, position, frames):
    pad = REACH * TPS
    padded = jnp.pad(tile_order, (pad, pad))
    near = lax.dynamic_slice_in_dim(padded, position * TPS, SPAN * TPS).reshape(SPAN, TPS)
    near_frames = position + jnp.arange(-REACH, REACH + 1, dtype=jnp.int32)[:, None]
    inside = (near_frames >= 0) & (near_frames < frames)
    spatial = near - near_frames * TPS
    spatial = jnp.where(near_frames >= frames // 2, traded(spatial), spatial)
    own = lax.dynamic_slice_in_dim(tile_order, position * TPS, TPS) - position * TPS
    own = jnp.where(position >= frames // 2, traded(own), own)
    rows = lax.dynamic_slice_in_dim(tile_mask, position * TPS, TPS, 0).reshape(TPS, SPAN, TPS)
    ids = jnp.arange(TPS, dtype=jnp.int32)
    pick_q = own[:, None] == ids
    pick_k = (spatial[:, :, None] == ids) & inside[:, :, None]
    hit = (
        pick_q[:, None, None, :, None]
        & pick_k[None, :, :, None, :]
        & (rows != 0).transpose(1, 0, 2)[None, :, None, :, :]
    )
    allowed = jnp.any(hit, axis=(3, 4))
    return jnp.where(allowed, 0.0, NEG).astype(jnp.float32).reshape(-1)


def partner(u, frame, frames):
    return u ^ 2 if frame >= frames // 2 and u % 2 else u


def traded(slots):
    return jnp.stack([slots[..., i ^ 2 if i % 2 else i] for i in range(TPS)], axis=-1)


def shifted(block, distance, frames, groups):
    route = []
    for i in range(frames):
        j = i + distance
        if 0 <= j < frames:
            for u in range(groups):
                to = partner(partner(u, i, frames), j, frames)
                route.append((i * groups + u, j * groups + to))
    return lax.ppermute(block, AXES, route)


def exchanged(x, frames, groups):
    places = [
        [f * groups + partner(p, f, frames) for p in range(groups)] for f in range(frames)
    ]
    return lax.all_to_all(
        x, AXES, split_axis=0, concat_axis=0, axis_index_groups=places, tiled=True
    )


def swapped(x, step, frames, groups):
    route = []
    for f in range(frames):
        for u in range(groups):
            to = partner(partner(u, f, frames) ^ step, f, frames)
            route.append((f * groups + u, f * groups + to))
    return lax.ppermute(x, AXES, route)


def after(x, *others):
    return lax.optimization_barrier((x, *others))[0]


def per_device(queries, keys, values, tile_order, tile_mask):
    groups = lax.axis_size("uly")
    frames = lax.axis_size("blk")
    position = lax.axis_index("blk")
    move = functools.partial(shifted, frames=frames, groups=groups)
    swap = functools.partial(exchanged, frames=frames, groups=groups)
    u = lax.axis_index("uly")
    place = jnp.where((position >= frames // 2) & (u % 2 == 1), u ^ 2, u).astype(jnp.int32).reshape(1)
    kv0 = pack_kv(keys, values, groups, CHUNKS[0], 0)
    kv1 = pack_kv(keys, values, groups, CHUNKS[1], CHUNKS[0])
    q = pack_q(queries, groups)
    bias = tile_bias(tile_order, tile_mask, position, frames)

    own0 = swap(kv0)
    up0, down0 = move(own0, 1), move(own0, -1)
    own1 = swap(after(kv1, own0))
    own_q = swap(after(q, own1))
    up1, down1 = move(own1, 1), move(own1, -1)
    up0b, down0b = move(up0, 1), move(down0, -1)
    up1b, down1b = move(up1, 1), move(down1, -1)
    part1 = attend(bias, place, own_q, {-1: up1, 0: own1, 1: down1}, CHUNKS[0], None, False)
    kvs0 = {-2: up0b, -1: up0, 0: own0, 1: down0, 2: down0b}
    out0 = attend(after(bias, part1[0]), place, own_q, kvs0, 0)
    res0 = swap(out0)
    out1 = attend(
        bias, place, own_q, {-2: up1b, 2: down1b}, CHUNKS[0], part1, spread=True
    )
    res1 = [out1[0]] + [
        swapped(out1[t], t, frames, groups) for t in (2, 3, 1)
    ]
    return unpack(place, res0, [res1[0], res1[3], res1[1], res1[2]])


def solution(mesh):
    return jax.shard_map(
        per_device,
        mesh=mesh,
        in_specs=(
            P(AXES, None),
            P(AXES, None),
            P(AXES, None),
            P(),
            P(),
        ),
        out_specs=P(AXES, None),
        check_vma=False,
    )
```

```python
import functools
import math

import jax
import jax.numpy as jnp
from jax import lax
from jax.experimental import pallas as pl
from jax.experimental.pallas import tpu as pltpu
from jax.sharding import PartitionSpec as P

HEAD = 128
TPS = 4
REACH = 2
SPAN = 2 * REACH + 1
CHUNKS = (3, 3)
NEG = -1e30
SMALL = 4 * 1024 * 1024
LARGE = 60 * 1024 * 1024
AXES = ("blk", "uly")


def run_copies(pairs, sems):
    copies = [pltpu.make_async_copy(src, dst, sems.at[i]) for i, (src, dst) in enumerate(pairs)]
    for copy in copies:
        copy.start()
    for copy in copies:
        copy.wait()


def relay(triples, sems):
    ins = [pltpu.make_async_copy(src, via, sems.at[i, 0]) for i, (src, via, _) in enumerate(triples)]
    outs = [pltpu.make_async_copy(via, dst, sems.at[i, 1]) for i, (_, via, dst) in enumerate(triples)]
    for copy in ins:
        copy.start()
    for first, second in zip(ins, outs):
        first.wait()
        second.start()
    for copy in outs:
        copy.wait()


def pack_kv_kernel(groups, skip, k_ref, v_ref, out_ref, via_ref, sems):
    width, cols = k_ref.shape[1] // groups, out_ref.shape[-1]
    triples = []
    for u in range(groups):
        at = pl.ds(u * width + skip * HEAD, cols)
        triples += [
            (ref.at[:, at], via_ref.at[u, i], out_ref.at[u, i])
            for i, ref in enumerate((k_ref, v_ref))
        ]
    relay(triples, sems)


def pack_kv(keys, values, groups, heads, skip):
    shape = (groups, 2, keys.shape[0], heads * HEAD)
    return pl.pallas_call(
        functools.partial(pack_kv_kernel, groups, skip),
        in_specs=[pl.BlockSpec(memory_space=pltpu.HBM)] * 2,
        out_specs=pl.BlockSpec(memory_space=pltpu.HBM),
        out_shape=jax.ShapeDtypeStruct(shape, jnp.bfloat16),
        scratch_shapes=[
            pltpu.VMEM(shape, jnp.bfloat16),
            pltpu.SemaphoreType.DMA((2 * groups, 2)),
        ],
        compiler_params=pltpu.CompilerParams(vmem_limit_bytes=LARGE),
        name="pack_kv",
    )(keys, values)


def pack_q_kernel(groups, q_ref, out_ref, via_ref, sems):
    width = q_ref.shape[1] // groups
    triples = [
        (q_ref.at[:, pl.ds(u * width, width)], via_ref.at[u], out_ref.at[u])
        for u in range(groups)
    ]
    relay(triples, sems)


def pack_q(queries, groups):
    shape = (groups, queries.shape[0], queries.shape[1] // groups)
    return pl.pallas_call(
        functools.partial(pack_q_kernel, groups),
        in_specs=[pl.BlockSpec(memory_space=pltpu.HBM)],
        out_specs=pl.BlockSpec(memory_space=pltpu.HBM),
        out_shape=jax.ShapeDtypeStruct(shape, jnp.bfloat16),
        scratch_shapes=[
            pltpu.VMEM(shape, jnp.bfloat16),
            pltpu.SemaphoreType.DMA((groups, 2)),
        ],
        compiler_params=pltpu.CompilerParams(vmem_limit_bytes=LARGE),
        name="pack_q",
    )(queries)


def unpack_kernel(groups, place_ref, first_ref, *refs):
    rest, out_ref, sems = refs[:groups], refs[groups], refs[groups + 1]
    width, cols = out_ref.shape[1] // groups, first_ref.shape[-1]
    place = place_ref[0]
    pairs = []
    for t in range(groups):
        start = pl.multiple_of((place ^ t) * width + cols, HEAD)
        pairs.append((rest[t], out_ref.at[:, pl.ds(start, width - cols)]))
    for u in range(groups):
        pairs.append((first_ref.at[u], out_ref.at[:, pl.ds(u * width, cols)]))
    run_copies(pairs, sems)


def unpack(place, first, rest):
    groups, rows, cols = first.shape
    width = groups * (cols + rest[0].shape[-1])
    return pl.pallas_call(
        functools.partial(unpack_kernel, groups),
        in_specs=[pl.BlockSpec(memory_space=pltpu.SMEM)]
        + [pl.BlockSpec(memory_space=pl.ANY)] * (1 + groups),
        out_shape=jax.ShapeDtypeStruct((rows, width), jnp.bfloat16),
        scratch_shapes=[pltpu.SemaphoreType.DMA((2 * groups,))],
        compiler_params=pltpu.CompilerParams(vmem_limit_bytes=SMALL),
        name="unpack",
    )(place, first, *rest)


def attend_kernel(scale, offsets, carried, final, spread, bias_ref, place_ref, q_ref, *refs):
    count = len(offsets)
    kv_refs, refs = refs[:count], refs[count:]
    s_ref, o_ref, refs = refs[-2], refs[-1], refs[:-2]
    rows = q_ref.shape[1]
    frame_rows = TPS * rows
    q = q_ref[...].reshape(frame_rows, HEAD)
    tops = [None] * TPS
    for i, offset in enumerate(offsets):
        e = offset + REACH
        k = kv_refs[i][:, 0].reshape(frame_rows, HEAD)
        s = lax.dot_general(k, q, (((1,), (1,)), ((), ())), preferred_element_type=jnp.float32)
        for b in range(TPS):
            for a in range(TPS):
                block = s[b * rows : (b + 1) * rows, a * rows : (a + 1) * rows]
                block = block + bias_ref[a * SPAN * TPS + e * TPS + b]
                s_ref[i * TPS + b, :, a * rows : (a + 1) * rows] = block
                top = jnp.max(block, axis=0, keepdims=True)
                tops[a] = top if tops[a] is None else jnp.maximum(tops[a], top)
    top = jnp.concatenate(tops, axis=1) * scale
    if carried:
        accum_ref, stats_ref = refs[:2]
        refs = refs[2:]
        before = stats_ref[0, 0:1]
        top = jnp.maximum(top, before)
        factor = jnp.exp2(before - top)
        total = stats_ref[0, 1:2] * factor
        accum = accum_ref[0] * factor
    else:
        total = jnp.zeros((1, frame_rows), jnp.float32)
        accum = None
    for i in range(count):
        s = s_ref[i * TPS : (i + 1) * TPS].reshape(frame_rows, frame_rows)
        w = jnp.exp2(s * scale - top)
        total = total + jnp.sum(w, axis=0, keepdims=True)
        v = kv_refs[i][:, 1].reshape(frame_rows, HEAD)
        part = lax.dot_general(
            v, w.astype(jnp.bfloat16), (((0,), (0,)), ((), ())), preferred_element_type=jnp.float32
        )
        accum = part if accum is None else accum + part
    if final:
        out = (accum / total).T.reshape(TPS, rows, HEAD).astype(jnp.bfloat16)
        if spread:
            o_ref[...] = out
            for t in range(TPS):
                refs[t][...] = o_ref[place_ref[0] ^ t]
        else:
            refs[0][...] = out
    else:
        refs[0][0] = accum
        refs[1][0, 0:1] = top
        refs[1][0, 1:2] = total


def attend(bias, place, q, kvs, first, carry=None, final=True, spread=False):
    offsets = sorted(kvs)
    groups, _, rows, cols = kvs[offsets[0]].shape
    heads = cols // HEAD
    queries = groups * rows
    keys = len(offsets) * queries
    kv_spec = pl.BlockSpec((groups, 2, rows, HEAD), lambda h: (0, 0, 0, h))
    state_specs = [
        pl.BlockSpec((1, HEAD, queries), lambda h: (h, 0, 0)),
        pl.BlockSpec((1, 2, queries), lambda h: (h, 0, 0)),
    ]
    if spread:
        out_specs = [pl.BlockSpec((rows, HEAD), lambda h: (0, h))] * groups
        out_shape = [jax.ShapeDtypeStruct((rows, cols), jnp.bfloat16)] * groups
    elif final:
        out_specs = pl.BlockSpec((groups, rows, HEAD), lambda h: (0, 0, h))
        out_shape = jax.ShapeDtypeStruct((groups, rows, cols), jnp.bfloat16)
    else:
        out_specs = state_specs
        out_shape = [
            jax.ShapeDtypeStruct((heads, HEAD, queries), jnp.float32),
            jax.ShapeDtypeStruct((heads, 2, queries), jnp.float32),
        ]
    return pl.pallas_call(
        functools.partial(
            attend_kernel,
            math.log2(math.e) / math.sqrt(HEAD),
            offsets,
            carry is not None,
            final,
            spread,
        ),
        grid=(heads,),
        in_specs=[
            pl.BlockSpec(memory_space=pltpu.SMEM),
            pl.BlockSpec(memory_space=pltpu.SMEM),
            pl.BlockSpec((groups, rows, HEAD), lambda h: (0, 0, h + first)),
        ]
        + [kv_spec] * len(offsets)
        + (state_specs if carry is not None else []),
        out_specs=out_specs,
        out_shape=out_shape,
        scratch_shapes=[
            pltpu.VMEM((len(offsets) * TPS, rows, queries), jnp.float32),
            pltpu.VMEM((TPS, rows, HEAD), jnp.bfloat16),
        ],
        compiler_params=pltpu.CompilerParams(vmem_limit_bytes=32 * 1024 * 1024),
        cost_estimate=pl.CostEstimate(
            flops=4 * heads * queries * keys * HEAD,
            bytes_accessed=2 * cols * (2 * queries + 2 * keys),
            transcendentals=heads * queries * keys,
        ),
        name="attend",
    )(bias, place, q, *[kvs[o] for o in offsets], *(carry or ()))


def tile_bias(tile_order, tile_mask, position, frames):
    pad = REACH * TPS
    padded = jnp.pad(tile_order, (pad, pad))
    near = lax.dynamic_slice_in_dim(padded, position * TPS, SPAN * TPS).reshape(SPAN, TPS)
    near_frames = position + jnp.arange(-REACH, REACH + 1, dtype=jnp.int32)[:, None]
    inside = (near_frames >= 0) & (near_frames < frames)
    spatial = near - near_frames * TPS
    spatial = jnp.where(near_frames >= frames // 2, traded(spatial), spatial)
    own = lax.dynamic_slice_in_dim(tile_order, position * TPS, TPS) - position * TPS
    own = jnp.where(position >= frames // 2, traded(own), own)
    rows = lax.dynamic_slice_in_dim(tile_mask, position * TPS, TPS, 0).reshape(TPS, SPAN, TPS)
    ids = jnp.arange(TPS, dtype=jnp.int32)
    pick_q = own[:, None] == ids
    pick_k = (spatial[:, :, None] == ids) & inside[:, :, None]
    hit = (
        pick_q[:, None, None, :, None]
        & pick_k[None, :, :, None, :]
        & (rows != 0).transpose(1, 0, 2)[None, :, None, :, :]
    )
    allowed = jnp.any(hit, axis=(3, 4))
    return jnp.where(allowed, 0.0, NEG).astype(jnp.float32).reshape(-1)


def partner(u, frame, frames):
    return u ^ 2 if frame >= frames // 2 and u % 2 else u


def traded(slots):
    return jnp.stack([slots[..., i ^ 2 if i % 2 else i] for i in range(TPS)], axis=-1)


def shifted(block, distance, frames, groups):
    route = []
    for i in range(frames):
        j = i + distance
        if 0 <= j < frames:
            for u in range(groups):
                to = partner(partner(u, i, frames), j, frames)
                route.append((i * groups + u, j * groups + to))
    return lax.ppermute(block, AXES, route)


def exchanged(x, frames, groups):
    places = [
        [f * groups + partner(p, f, frames) for p in range(groups)] for f in range(frames)
    ]
    return lax.all_to_all(
        x, AXES, split_axis=0, concat_axis=0, axis_index_groups=places, tiled=True
    )


def swapped(x, step, frames, groups):
    route = []
    for f in range(frames):
        for u in range(groups):
            to = partner(partner(u, f, frames) ^ step, f, frames)
            route.append((f * groups + u, f * groups + to))
    return lax.ppermute(x, AXES, route)


def after(x, *others):
    return lax.optimization_barrier((x, *others))[0]


def per_device(queries, keys, values, tile_order, tile_mask):
    groups = lax.axis_size("uly")
    frames = lax.axis_size("blk")
    position = lax.axis_index("blk")
    move = functools.partial(shifted, frames=frames, groups=groups)
    swap = functools.partial(exchanged, frames=frames, groups=groups)
    u = lax.axis_index("uly")
    place = jnp.where((position >= frames // 2) & (u % 2 == 1), u ^ 2, u).astype(jnp.int32).reshape(1)
    kv0 = pack_kv(keys, values, groups, CHUNKS[0], 0)
    kv1 = pack_kv(keys, values, groups, CHUNKS[1], CHUNKS[0])
    q = pack_q(queries, groups)
    bias = tile_bias(tile_order, tile_mask, position, frames)

    own0 = swap(kv0)
    up0, down0 = move(own0, 1), move(own0, -1)
    own1 = swap(after(kv1, own0))
    own_q = swap(after(q, own1))
    up1, down1 = move(own1, 1), move(own1, -1)
    up0b, down0b = move(up0, 1), move(down0, -1)
    up1b, down1b = move(up1, 1), move(down1, -1)
    part1 = attend(bias, place, own_q, {-1: up1, 0: own1, 1: down1}, CHUNKS[0], None, False)
    bias0 = after(bias, part1[0])
    part0 = attend(bias0, place, own_q, {-1: up0, 0: own0, 1: down0}, 0, None, False)
    out0 = attend(after(bias0, part0[0]), place, own_q, {-2: up0b, 2: down0b}, 0, part0)
    res0 = swap(out0)
    bias1 = after(bias, out0)
    out1 = attend(bias1, place, own_q, {-2: up1b, 2: down1b}, CHUNKS[0], part1, spread=True)
    res1 = [out1[0]] + [
        swapped(out1[t], t, frames, groups) for t in (2, 3, 1)
    ]
    return unpack(place, res0, [res1[0], res1[3], res1[1], res1[2]])


def solution(mesh):
    return jax.shard_map(
        per_device,
        mesh=mesh,
        in_specs=(
            P(AXES, None),
            P(AXES, None),
            P(AXES, None),
            P(),
            P(),
        ),
        out_specs=P(AXES, None),
        check_vma=False,
    )
```

```python
import functools
import math

import jax
import jax.numpy as jnp
from jax import lax
from jax.experimental import pallas as pl
from jax.experimental.pallas import tpu as pltpu
from jax.sharding import PartitionSpec as P

HEAD = 128
TPS = 4
REACH = 2
SPAN = 2 * REACH + 1
CHUNKS = (3, 3)
NEG = -1e30
SMALL = 4 * 1024 * 1024
LARGE = 60 * 1024 * 1024
AXES = ("blk", "uly")


def run_copies(pairs, sems):
    copies = [pltpu.make_async_copy(src, dst, sems.at[i]) for i, (src, dst) in enumerate(pairs)]
    for copy in copies:
        copy.start()
    for copy in copies:
        copy.wait()


def relay(triples, sems):
    ins = [pltpu.make_async_copy(src, via, sems.at[i, 0]) for i, (src, via, _) in enumerate(triples)]
    outs = [pltpu.make_async_copy(via, dst, sems.at[i, 1]) for i, (_, via, dst) in enumerate(triples)]
    for copy in ins:
        copy.start()
    for first, second in zip(ins, outs):
        first.wait()
        second.start()
    for copy in outs:
        copy.wait()


def pack_kv_kernel(groups, skip, k_ref, v_ref, out_ref, via_ref, sems):
    width, cols = k_ref.shape[1] // groups, out_ref.shape[-1]
    triples = []
    for u in range(groups):
        at = pl.ds(u * width + skip * HEAD, cols)
        triples += [
            (ref.at[:, at], via_ref.at[u, i], out_ref.at[u, i])
            for i, ref in enumerate((k_ref, v_ref))
        ]
    relay(triples, sems)


def pack_kv(keys, values, groups, heads, skip):
    shape = (groups, 2, keys.shape[0], heads * HEAD)
    return pl.pallas_call(
        functools.partial(pack_kv_kernel, groups, skip),
        in_specs=[pl.BlockSpec(memory_space=pltpu.HBM)] * 2,
        out_specs=pl.BlockSpec(memory_space=pltpu.HBM),
        out_shape=jax.ShapeDtypeStruct(shape, jnp.bfloat16),
        scratch_shapes=[
            pltpu.VMEM(shape, jnp.bfloat16),
            pltpu.SemaphoreType.DMA((2 * groups, 2)),
        ],
        compiler_params=pltpu.CompilerParams(vmem_limit_bytes=LARGE),
        name="pack_kv",
    )(keys, values)


def pack_q_kernel(groups, q_ref, out_ref, via_ref, sems):
    width = q_ref.shape[1] // groups
    triples = [
        (q_ref.at[:, pl.ds(u * width, width)], via_ref.at[u], out_ref.at[u])
        for u in range(groups)
    ]
    relay(triples, sems)


def pack_q(queries, groups):
    shape = (groups, queries.shape[0], queries.shape[1] // groups)
    return pl.pallas_call(
        functools.partial(pack_q_kernel, groups),
        in_specs=[pl.BlockSpec(memory_space=pltpu.HBM)],
        out_specs=pl.BlockSpec(memory_space=pltpu.HBM),
        out_shape=jax.ShapeDtypeStruct(shape, jnp.bfloat16),
        scratch_shapes=[
            pltpu.VMEM(shape, jnp.bfloat16),
            pltpu.SemaphoreType.DMA((groups, 2)),
        ],
        compiler_params=pltpu.CompilerParams(vmem_limit_bytes=LARGE),
        name="pack_q",
    )(queries)


def unpack_kernel(groups, place_ref, first_ref, *refs):
    rest, out_ref, sems = refs[:groups], refs[groups], refs[groups + 1]
    width, cols = out_ref.shape[1] // groups, first_ref.shape[-1]
    place = place_ref[0]
    pairs = []
    for t in range(groups):
        start = pl.multiple_of((place ^ t) * width + cols, HEAD)
        pairs.append((rest[t], out_ref.at[:, pl.ds(start, width - cols)]))
    for u in range(groups):
        pairs.append((first_ref.at[u], out_ref.at[:, pl.ds(u * width, cols)]))
    run_copies(pairs, sems)


def unpack(place, first, rest):
    groups, rows, cols = first.shape
    width = groups * (cols + rest[0].shape[-1])
    return pl.pallas_call(
        functools.partial(unpack_kernel, groups),
        in_specs=[pl.BlockSpec(memory_space=pltpu.SMEM)]
        + [pl.BlockSpec(memory_space=pl.ANY)] * (1 + groups),
        out_shape=jax.ShapeDtypeStruct((rows, width), jnp.bfloat16),
        scratch_shapes=[pltpu.SemaphoreType.DMA((2 * groups,))],
        compiler_params=pltpu.CompilerParams(vmem_limit_bytes=SMALL),
        name="unpack",
    )(place, first, *rest)


def attend_kernel(scale, offsets, carried, final, spread, first, bias_ref, place_ref, q_ref, *refs):
    count = len(offsets)
    kv_refs, refs = refs[:count], refs[count:]
    s_ref, o_ref, refs = refs[-2], refs[-1], refs[:-2]
    rows = q_ref.shape[1]
    frame_rows = TPS * rows
    if carried:
        accum_ref, stats_ref = refs[:2]
        refs = refs[2:]
    for h in range(kv_refs[0].shape[-1] // HEAD):
        at = slice(h * HEAD, (h + 1) * HEAD)
        q_at = slice((first + h) * HEAD, (first + h + 1) * HEAD)
        q = q_ref[:, :, q_at].reshape(frame_rows, HEAD)
        tops = [None] * TPS
        for i, offset in enumerate(offsets):
            e = offset + REACH
            k = kv_refs[i][:, 0, :, at].reshape(frame_rows, HEAD)
            s = lax.dot_general(
                k, q, (((1,), (1,)), ((), ())), preferred_element_type=jnp.float32
            )
            for b in range(TPS):
                for a in range(TPS):
                    block = s[b * rows : (b + 1) * rows, a * rows : (a + 1) * rows]
                    block = block + bias_ref[a * SPAN * TPS + e * TPS + b]
                    s_ref[0, i * TPS + b, :, a * rows : (a + 1) * rows] = block
                    top = jnp.max(block, axis=0, keepdims=True)
                    tops[a] = top if tops[a] is None else jnp.maximum(tops[a], top)
        top = jnp.concatenate(tops, axis=1) * scale
        if carried:
            before = stats_ref[h, 0:1]
            top = jnp.maximum(top, before)
            factor = jnp.exp2(before - top)
            total = stats_ref[h, 1:2] * factor
            accum = accum_ref[h] * factor
        else:
            total = jnp.zeros((1, frame_rows), jnp.float32)
            accum = None
        for i in range(count):
            s = s_ref[0, i * TPS : (i + 1) * TPS].reshape(frame_rows, frame_rows)
            w = jnp.exp2(s * scale - top)
            total = total + jnp.sum(w, axis=0, keepdims=True)
            v = kv_refs[i][:, 1, :, at].reshape(frame_rows, HEAD)
            part = lax.dot_general(
                v,
                w.astype(jnp.bfloat16),
                (((0,), (0,)), ((), ())),
                preferred_element_type=jnp.float32,
            )
            accum = part if accum is None else accum + part
        if final:
            out = (accum / total).T.reshape(TPS, rows, HEAD).astype(jnp.bfloat16)
            if spread:
                o_ref[h % 2] = out
                for t in range(TPS):
                    refs[t][:, at] = o_ref[h % 2, place_ref[0] ^ t]
            else:
                refs[0][:, :, at] = out
        else:
            refs[0][h] = accum
            refs[1][h, 0:1] = top
            refs[1][h, 1:2] = total


def attend(bias, place, q, kvs, first, carry=None, final=True, spread=False):
    offsets = sorted(kvs)
    groups, _, rows, cols = kvs[offsets[0]].shape
    heads = cols // HEAD
    queries = groups * rows
    keys = len(offsets) * queries
    if spread:
        out_shape = [jax.ShapeDtypeStruct((rows, cols), jnp.bfloat16)] * groups
    elif final:
        out_shape = jax.ShapeDtypeStruct((groups, rows, cols), jnp.bfloat16)
    else:
        out_shape = [
            jax.ShapeDtypeStruct((heads, HEAD, queries), jnp.float32),
            jax.ShapeDtypeStruct((heads, 2, queries), jnp.float32),
        ]
    whole = pl.BlockSpec(memory_space=pltpu.VMEM)
    arrays = [q] + [kvs[o] for o in offsets] + list(carry or ())
    return pl.pallas_call(
        functools.partial(
            attend_kernel,
            math.log2(math.e) / math.sqrt(HEAD),
            offsets,
            carry is not None,
            final,
            spread,
            first,
        ),
        in_specs=[pl.BlockSpec(memory_space=pltpu.SMEM)] * 2 + [whole] * len(arrays),
        out_shape=out_shape,
        out_specs=jax.tree.map(lambda _: whole, out_shape),
        scratch_shapes=[
            pltpu.VMEM((1, len(offsets) * TPS, rows, queries), jnp.float32),
            pltpu.VMEM((2, TPS, rows, HEAD), jnp.bfloat16),
        ],
        compiler_params=pltpu.CompilerParams(
            vmem_limit_bytes=(6 + 2 * len(offsets)) * 1024 * 1024
        ),
        cost_estimate=pl.CostEstimate(
            flops=4 * heads * queries * keys * HEAD,
            bytes_accessed=2 * cols * (2 * queries + 2 * keys),
            transcendentals=heads * queries * keys,
        ),
        name="attend",
    )(bias, place, *arrays)


def tile_bias(tile_order, tile_mask, position, frames):
    pad = REACH * TPS
    padded = jnp.pad(tile_order, (pad, pad))
    near = lax.dynamic_slice_in_dim(padded, position * TPS, SPAN * TPS).reshape(SPAN, TPS)
    near_frames = position + jnp.arange(-REACH, REACH + 1, dtype=jnp.int32)[:, None]
    inside = (near_frames >= 0) & (near_frames < frames)
    spatial = near - near_frames * TPS
    spatial = jnp.where(near_frames >= frames // 2, traded(spatial), spatial)
    own = lax.dynamic_slice_in_dim(tile_order, position * TPS, TPS) - position * TPS
    own = jnp.where(position >= frames // 2, traded(own), own)
    rows = lax.dynamic_slice_in_dim(tile_mask, position * TPS, TPS, 0).reshape(TPS, SPAN, TPS)
    ids = jnp.arange(TPS, dtype=jnp.int32)
    pick_q = own[:, None] == ids
    pick_k = (spatial[:, :, None] == ids) & inside[:, :, None]
    hit = (
        pick_q[:, None, None, :, None]
        & pick_k[None, :, :, None, :]
        & (rows != 0).transpose(1, 0, 2)[None, :, None, :, :]
    )
    allowed = jnp.any(hit, axis=(3, 4))
    return jnp.where(allowed, 0.0, NEG).astype(jnp.float32).reshape(-1)


def partner(u, frame, frames):
    return u ^ 2 if frame >= frames // 2 and u % 2 else u


def traded(slots):
    return jnp.stack([slots[..., i ^ 2 if i % 2 else i] for i in range(TPS)], axis=-1)


def shifted(block, distance, frames, groups):
    route = []
    for i in range(frames):
        j = i + distance
        if 0 <= j < frames:
            for u in range(groups):
                to = partner(partner(u, i, frames), j, frames)
                route.append((i * groups + u, j * groups + to))
    return lax.ppermute(block, AXES, route)


def exchanged(x, frames, groups):
    places = [
        [f * groups + partner(p, f, frames) for p in range(groups)] for f in range(frames)
    ]
    return lax.all_to_all(
        x, AXES, split_axis=0, concat_axis=0, axis_index_groups=places, tiled=True
    )


def swapped(x, step, frames, groups):
    route = []
    for f in range(frames):
        for u in range(groups):
            to = partner(partner(u, f, frames) ^ step, f, frames)
            route.append((f * groups + u, f * groups + to))
    return lax.ppermute(x, AXES, route)


def after(x, *others):
    return lax.optimization_barrier((x, *others))[0]


def per_device(queries, keys, values, tile_order, tile_mask):
    groups = lax.axis_size("uly")
    frames = lax.axis_size("blk")
    position = lax.axis_index("blk")
    move = functools.partial(shifted, frames=frames, groups=groups)
    swap = functools.partial(exchanged, frames=frames, groups=groups)
    u = lax.axis_index("uly")
    place = jnp.where((position >= frames // 2) & (u % 2 == 1), u ^ 2, u).astype(jnp.int32).reshape(1)
    kv0 = pack_kv(keys, values, groups, CHUNKS[0], 0)
    kv1 = pack_kv(keys, values, groups, CHUNKS[1], CHUNKS[0])
    q = pack_q(queries, groups)
    bias = tile_bias(tile_order, tile_mask, position, frames)

    own0 = swap(kv0)
    up0, down0 = move(own0, 1), move(own0, -1)
    own1 = swap(after(kv1, own0))
    own_q = swap(after(q, own1))
    up1, down1 = move(own1, 1), move(own1, -1)
    up0b, down0b = move(up0, 1), move(down0, -1)
    up1b, down1b = move(up1, 1), move(down1, -1)
    part1 = attend(bias, place, own_q, {-1: up1, 0: own1, 1: down1}, CHUNKS[0], None, False)
    bias0 = after(bias, part1[0])
    part0 = attend(bias0, place, own_q, {-1: up0, 0: own0, 1: down0}, 0, None, False)
    out0 = attend(after(bias0, part0[0]), place, own_q, {-2: up0b, 2: down0b}, 0, part0)
    res0 = swap(out0)
    bias1 = after(bias, out0)
    part1 = attend(bias1, place, own_q, {-2: up1b}, CHUNKS[0], part1, False)
    bias1 = after(bias1, part1[0])
    out1 = attend(bias1, place, own_q, {2: down1b}, CHUNKS[0], part1, spread=True)
    res1 = [out1[0]] + [
        swapped(out1[t], t, frames, groups) for t in (2, 3, 1)
    ]
    return unpack(place, res0, [res1[0], res1[3], res1[1], res1[2]])


def solution(mesh):
    return jax.shard_map(
        per_device,
        mesh=mesh,
        in_specs=(
            P(AXES, None),
            P(AXES, None),
            P(AXES, None),
            P(),
            P(),
        ),
        out_specs=P(AXES, None),
        check_vma=False,
    )
```

```python
import functools
import math

import jax
import jax.numpy as jnp
from jax import lax
from jax.experimental import pallas as pl
from jax.experimental.pallas import tpu as pltpu
from jax.sharding import PartitionSpec as P

HEAD = 128
TPS = 4
REACH = 2
SPAN = 2 * REACH + 1
CHUNKS = (3, 3)
NEG = -1e30
SMALL = 4 * 1024 * 1024
LARGE = 60 * 1024 * 1024
AXES = ("blk", "uly")


def run_copies(pairs, sems):
    copies = [pltpu.make_async_copy(src, dst, sems.at[i]) for i, (src, dst) in enumerate(pairs)]
    for copy in copies:
        copy.start()
    for copy in copies:
        copy.wait()


def relay(triples, sems):
    ins = [pltpu.make_async_copy(src, via, sems.at[i, 0]) for i, (src, via, _) in enumerate(triples)]
    outs = [pltpu.make_async_copy(via, dst, sems.at[i, 1]) for i, (_, via, dst) in enumerate(triples)]
    for copy in ins:
        copy.start()
    for first, second in zip(ins, outs):
        first.wait()
        second.start()
    for copy in outs:
        copy.wait()


def pack_kv_kernel(groups, skip, k_ref, v_ref, out_ref, via_ref, sems):
    width, cols = k_ref.shape[1] // groups, out_ref.shape[-1]
    triples = []
    for u in range(groups):
        at = pl.ds(u * width + skip * HEAD, cols)
        triples += [
            (ref.at[:, at], via_ref.at[u, i], out_ref.at[u, i])
            for i, ref in enumerate((k_ref, v_ref))
        ]
    relay(triples, sems)


def pack_kv(keys, values, groups, heads, skip):
    shape = (groups, 2, keys.shape[0], heads * HEAD)
    return pl.pallas_call(
        functools.partial(pack_kv_kernel, groups, skip),
        in_specs=[pl.BlockSpec(memory_space=pltpu.HBM)] * 2,
        out_specs=pl.BlockSpec(memory_space=pltpu.HBM),
        out_shape=jax.ShapeDtypeStruct(shape, jnp.bfloat16),
        scratch_shapes=[
            pltpu.VMEM(shape, jnp.bfloat16),
            pltpu.SemaphoreType.DMA((2 * groups, 2)),
        ],
        compiler_params=pltpu.CompilerParams(vmem_limit_bytes=LARGE),
        name="pack_kv",
    )(keys, values)


def pack_q_kernel(groups, q_ref, out_ref, via_ref, sems):
    width = q_ref.shape[1] // groups
    triples = [
        (q_ref.at[:, pl.ds(u * width, width)], via_ref.at[u], out_ref.at[u])
        for u in range(groups)
    ]
    relay(triples, sems)


def pack_q(queries, groups):
    shape = (groups, queries.shape[0], queries.shape[1] // groups)
    return pl.pallas_call(
        functools.partial(pack_q_kernel, groups),
        in_specs=[pl.BlockSpec(memory_space=pltpu.HBM)],
        out_specs=pl.BlockSpec(memory_space=pltpu.HBM),
        out_shape=jax.ShapeDtypeStruct(shape, jnp.bfloat16),
        scratch_shapes=[
            pltpu.VMEM(shape, jnp.bfloat16),
            pltpu.SemaphoreType.DMA((groups, 2)),
        ],
        compiler_params=pltpu.CompilerParams(vmem_limit_bytes=LARGE),
        name="pack_q",
    )(queries)


def unpack_kernel(groups, place_ref, *refs):
    pieces, out_ref, sems = refs[:-2], refs[-2], refs[-1]
    width = out_ref.shape[1] // groups
    pairs, first = [], 0
    for c in range(len(pieces) // groups):
        cols = pieces[c * groups].shape[-1]
        for t in range(groups):
            start = pl.multiple_of((place_ref[0] ^ t) * width + first, HEAD)
            pairs.append((pieces[c * groups + t], out_ref.at[:, pl.ds(start, cols)]))
        first += cols
    run_copies(pairs, sems)


def unpack(place, chunks):
    groups, rows = len(chunks[0]), chunks[0][0].shape[0]
    width = groups * sum(c[0].shape[-1] for c in chunks)
    pieces = [p for c in chunks for p in c]
    return pl.pallas_call(
        functools.partial(unpack_kernel, groups),
        in_specs=[pl.BlockSpec(memory_space=pltpu.SMEM)]
        + [pl.BlockSpec(memory_space=pl.ANY)] * len(pieces),
        out_shape=jax.ShapeDtypeStruct((rows, width), jnp.bfloat16),
        scratch_shapes=[pltpu.SemaphoreType.DMA((len(pieces),))],
        compiler_params=pltpu.CompilerParams(vmem_limit_bytes=SMALL),
        name="unpack",
    )(place, *pieces)


def attend_kernel(scale, offsets, carried, final, spread, first, bias_ref, place_ref, q_ref, *refs):
    count = len(offsets)
    kv_refs, refs = refs[:count], refs[count:]
    s_ref, o_ref, refs = refs[-2], refs[-1], refs[:-2]
    rows = q_ref.shape[1]
    frame_rows = TPS * rows
    if carried:
        accum_ref, stats_ref = refs[:2]
        refs = refs[2:]
    for h in range(kv_refs[0].shape[-1] // HEAD):
        at = slice(h * HEAD, (h + 1) * HEAD)
        q_at = slice((first + h) * HEAD, (first + h + 1) * HEAD)
        q = q_ref[:, :, q_at].reshape(frame_rows, HEAD)
        tops = [None] * TPS
        for i, offset in enumerate(offsets):
            e = offset + REACH
            k = kv_refs[i][:, 0, :, at].reshape(frame_rows, HEAD)
            s = lax.dot_general(
                k, q, (((1,), (1,)), ((), ())), preferred_element_type=jnp.float32
            )
            for b in range(TPS):
                for a in range(TPS):
                    block = s[b * rows : (b + 1) * rows, a * rows : (a + 1) * rows]
                    block = block + bias_ref[a * SPAN * TPS + e * TPS + b]
                    s_ref[0, i * TPS + b, :, a * rows : (a + 1) * rows] = block
                    top = jnp.max(block, axis=0, keepdims=True)
                    tops[a] = top if tops[a] is None else jnp.maximum(tops[a], top)
        top = jnp.concatenate(tops, axis=1) * scale
        if carried:
            before = stats_ref[h, 0:1]
            top = jnp.maximum(top, before)
            factor = jnp.exp2(before - top)
            total = stats_ref[h, 1:2] * factor
            accum = accum_ref[h] * factor
        else:
            total = jnp.zeros((1, frame_rows), jnp.float32)
            accum = None
        for i in range(count):
            s = s_ref[0, i * TPS : (i + 1) * TPS].reshape(frame_rows, frame_rows)
            w = jnp.exp2(s * scale - top)
            total = total + jnp.sum(w, axis=0, keepdims=True)
            v = kv_refs[i][:, 1, :, at].reshape(frame_rows, HEAD)
            part = lax.dot_general(
                v,
                w.astype(jnp.bfloat16),
                (((0,), (0,)), ((), ())),
                preferred_element_type=jnp.float32,
            )
            accum = part if accum is None else accum + part
        if final:
            out = (accum / total).T.reshape(TPS, rows, HEAD).astype(jnp.bfloat16)
            if spread:
                o_ref[h % 2] = out
                for t in range(TPS):
                    refs[t][:, at] = o_ref[h % 2, place_ref[0] ^ t]
            else:
                refs[0][:, :, at] = out
        else:
            refs[0][h] = accum
            refs[1][h, 0:1] = top
            refs[1][h, 1:2] = total


def attend(bias, place, q, kvs, first, carry=None, final=True, spread=False):
    offsets = sorted(kvs)
    groups, _, rows, cols = kvs[offsets[0]].shape
    heads = cols // HEAD
    queries = groups * rows
    keys = len(offsets) * queries
    if spread:
        out_shape = [jax.ShapeDtypeStruct((rows, cols), jnp.bfloat16)] * groups
    elif final:
        out_shape = jax.ShapeDtypeStruct((groups, rows, cols), jnp.bfloat16)
    else:
        out_shape = [
            jax.ShapeDtypeStruct((heads, HEAD, queries), jnp.float32),
            jax.ShapeDtypeStruct((heads, 2, queries), jnp.float32),
        ]
    whole = pl.BlockSpec(memory_space=pltpu.VMEM)
    arrays = [q] + [kvs[o] for o in offsets] + list(carry or ())
    return pl.pallas_call(
        functools.partial(
            attend_kernel,
            math.log2(math.e) / math.sqrt(HEAD),
            offsets,
            carry is not None,
            final,
            spread,
            first,
        ),
        in_specs=[pl.BlockSpec(memory_space=pltpu.SMEM)] * 2 + [whole] * len(arrays),
        out_shape=out_shape,
        out_specs=jax.tree.map(lambda _: whole, out_shape),
        scratch_shapes=[
            pltpu.VMEM((1, len(offsets) * TPS, rows, queries), jnp.float32),
            pltpu.VMEM((2, TPS, rows, HEAD), jnp.bfloat16),
        ],
        compiler_params=pltpu.CompilerParams(
            vmem_limit_bytes=(6 + 2 * len(offsets)) * 1024 * 1024
        ),
        cost_estimate=pl.CostEstimate(
            flops=4 * heads * queries * keys * HEAD,
            bytes_accessed=2 * cols * (2 * queries + 2 * keys),
            transcendentals=heads * queries * keys,
        ),
        name="attend",
    )(bias, place, *arrays)


def tile_bias(tile_order, tile_mask, position, frames):
    pad = REACH * TPS
    padded = jnp.pad(tile_order, (pad, pad))
    near = lax.dynamic_slice_in_dim(padded, position * TPS, SPAN * TPS).reshape(SPAN, TPS)
    near_frames = position + jnp.arange(-REACH, REACH + 1, dtype=jnp.int32)[:, None]
    inside = (near_frames >= 0) & (near_frames < frames)
    spatial = near - near_frames * TPS
    spatial = jnp.where(near_frames >= frames // 2, traded(spatial), spatial)
    own = lax.dynamic_slice_in_dim(tile_order, position * TPS, TPS) - position * TPS
    own = jnp.where(position >= frames // 2, traded(own), own)
    rows = lax.dynamic_slice_in_dim(tile_mask, position * TPS, TPS, 0).reshape(TPS, SPAN, TPS)
    ids = jnp.arange(TPS, dtype=jnp.int32)
    pick_q = own[:, None] == ids
    pick_k = (spatial[:, :, None] == ids) & inside[:, :, None]
    hit = (
        pick_q[:, None, None, :, None]
        & pick_k[None, :, :, None, :]
        & (rows != 0).transpose(1, 0, 2)[None, :, None, :, :]
    )
    allowed = jnp.any(hit, axis=(3, 4))
    return jnp.where(allowed, 0.0, NEG).astype(jnp.float32).reshape(-1)


def partner(u, frame, frames):
    return u ^ 2 if frame >= frames // 2 and u % 2 else u


def traded(slots):
    return jnp.stack([slots[..., i ^ 2 if i % 2 else i] for i in range(TPS)], axis=-1)


def shifted(block, distance, frames, groups):
    route = []
    for i in range(frames):
        j = i + distance
        if 0 <= j < frames:
            for u in range(groups):
                to = partner(partner(u, i, frames), j, frames)
                route.append((i * groups + u, j * groups + to))
    return lax.ppermute(block, AXES, route)


def exchanged(x, frames, groups):
    places = [
        [f * groups + partner(p, f, frames) for p in range(groups)] for f in range(frames)
    ]
    return lax.all_to_all(
        x, AXES, split_axis=0, concat_axis=0, axis_index_groups=places, tiled=True
    )


def swapped(x, step, frames, groups):
    route = []
    for f in range(frames):
        for u in range(groups):
            to = partner(partner(u, f, frames) ^ step, f, frames)
            route.append((f * groups + u, f * groups + to))
    return lax.ppermute(x, AXES, route)


def after(x, *others):
    return lax.optimization_barrier((x, *others))[0]


def per_device(queries, keys, values, tile_order, tile_mask):
    groups = lax.axis_size("uly")
    frames = lax.axis_size("blk")
    position = lax.axis_index("blk")
    move = functools.partial(shifted, frames=frames, groups=groups)
    def spread_out(parts):
        moved = {t: swapped(parts[t], t, frames, groups) for t in (2, 3, 1)}
        return [parts[0]] + [moved[t] for t in (1, 2, 3)]

    swap = functools.partial(exchanged, frames=frames, groups=groups)
    u = lax.axis_index("uly")
    place = jnp.where((position >= frames // 2) & (u % 2 == 1), u ^ 2, u).astype(jnp.int32).reshape(1)
    kv0 = pack_kv(keys, values, groups, CHUNKS[0], 0)
    kv1 = pack_kv(keys, values, groups, CHUNKS[1], CHUNKS[0])
    q = pack_q(queries, groups)
    bias = tile_bias(tile_order, tile_mask, position, frames)

    own0 = swap(kv0)
    up0, down0 = move(own0, 1), move(own0, -1)
    own1 = swap(after(kv1, own0))
    own_q = swap(after(q, own1))
    up1, down1 = move(own1, 1), move(own1, -1)
    up0b, down0b = move(up0, 1), move(down0, -1)
    up1b, down1b = move(up1, 1), move(down1, -1)
    part1 = attend(bias, place, own_q, {-1: up1, 0: own1, 1: down1}, CHUNKS[0], None, False)
    bias0 = after(bias, part1[0])
    part0 = attend(bias0, place, own_q, {-1: up0, 0: own0, 1: down0}, 0, None, False)
    out0 = attend(after(bias0, part0[0]), place, own_q, {-2: up0b, 2: down0b}, 0, part0, spread=True)
    res0 = spread_out(out0)
    bias1 = after(bias, out0[0])
    part1 = attend(bias1, place, own_q, {-2: up1b}, CHUNKS[0], part1, False)
    bias1 = after(bias1, part1[0])
    out1 = attend(bias1, place, own_q, {2: down1b}, CHUNKS[0], part1, spread=True)
    return unpack(place, [res0, spread_out(out1)])


def solution(mesh):
    return jax.shard_map(
        per_device,
        mesh=mesh,
        in_specs=(
            P(AXES, None),
            P(AXES, None),
            P(AXES, None),
            P(),
            P(),
        ),
        out_specs=P(AXES, None),
        check_vma=False,
    )
```

```python
import functools
import math

import jax
import jax.numpy as jnp
from jax import lax
from jax.experimental import pallas as pl
from jax.experimental.pallas import tpu as pltpu
from jax.sharding import PartitionSpec as P

HEAD = 128
TPS = 4
REACH = 2
SPAN = 2 * REACH + 1
CHUNKS = (3, 3)
NEG = -1e30
SMALL = 4 * 1024 * 1024
LARGE = 60 * 1024 * 1024
AXES = ("blk", "uly")


def run_copies(pairs, sems):
    copies = [pltpu.make_async_copy(src, dst, sems.at[i]) for i, (src, dst) in enumerate(pairs)]
    for copy in copies:
        copy.start()
    for copy in copies:
        copy.wait()


def relay(triples, sems):
    ins = [pltpu.make_async_copy(src, via, sems.at[i, 0]) for i, (src, via, _) in enumerate(triples)]
    outs = [pltpu.make_async_copy(via, dst, sems.at[i, 1]) for i, (_, via, dst) in enumerate(triples)]
    for copy in ins:
        copy.start()
    for first, second in zip(ins, outs):
        first.wait()
        second.start()
    for copy in outs:
        copy.wait()


def pack_kv_kernel(groups, skip, k_ref, v_ref, out_ref, via_ref, sems):
    width, cols = k_ref.shape[1] // groups, out_ref.shape[-1]
    triples = []
    for u in range(groups):
        at = pl.ds(u * width + skip * HEAD, cols)
        triples += [
            (ref.at[:, at], via_ref.at[u, i], out_ref.at[u, i])
            for i, ref in enumerate((k_ref, v_ref))
        ]
    relay(triples, sems)


def pack_kv(keys, values, groups, heads, skip):
    shape = (groups, 2, keys.shape[0], heads * HEAD)
    return pl.pallas_call(
        functools.partial(pack_kv_kernel, groups, skip),
        in_specs=[pl.BlockSpec(memory_space=pltpu.HBM)] * 2,
        out_specs=pl.BlockSpec(memory_space=pltpu.HBM),
        out_shape=jax.ShapeDtypeStruct(shape, jnp.bfloat16),
        scratch_shapes=[
            pltpu.VMEM(shape, jnp.bfloat16),
            pltpu.SemaphoreType.DMA((2 * groups, 2)),
        ],
        compiler_params=pltpu.CompilerParams(vmem_limit_bytes=LARGE),
        name="pack_kv",
    )(keys, values)


def pack_q_kernel(groups, q_ref, out_ref, via_ref, sems):
    width = q_ref.shape[1] // groups
    triples = [
        (q_ref.at[:, pl.ds(u * width, width)], via_ref.at[u], out_ref.at[u])
        for u in range(groups)
    ]
    relay(triples, sems)


def pack_q(queries, groups):
    shape = (groups, queries.shape[0], queries.shape[1] // groups)
    return pl.pallas_call(
        functools.partial(pack_q_kernel, groups),
        in_specs=[pl.BlockSpec(memory_space=pltpu.HBM)],
        out_specs=pl.BlockSpec(memory_space=pltpu.HBM),
        out_shape=jax.ShapeDtypeStruct(shape, jnp.bfloat16),
        scratch_shapes=[
            pltpu.VMEM(shape, jnp.bfloat16),
            pltpu.SemaphoreType.DMA((groups, 2)),
        ],
        compiler_params=pltpu.CompilerParams(vmem_limit_bytes=LARGE),
        name="pack_q",
    )(queries)


def unpack_kernel(groups, place_ref, *refs):
    pieces, out_ref, sems = refs[:-2], refs[-2], refs[-1]
    width = out_ref.shape[1] // groups
    pairs, first = [], 0
    for c in range(len(pieces) // groups):
        cols = pieces[c * groups].shape[-1]
        for t in range(groups):
            start = pl.multiple_of((place_ref[0] ^ t) * width + first, HEAD)
            pairs.append((pieces[c * groups + t], out_ref.at[:, pl.ds(start, cols)]))
        first += cols
    run_copies(pairs, sems)


def unpack(place, chunks):
    groups, rows = len(chunks[0]), chunks[0][0].shape[0]
    width = groups * sum(c[0].shape[-1] for c in chunks)
    pieces = [p for c in chunks for p in c]
    return pl.pallas_call(
        functools.partial(unpack_kernel, groups),
        in_specs=[pl.BlockSpec(memory_space=pltpu.SMEM)]
        + [pl.BlockSpec(memory_space=pl.ANY)] * len(pieces),
        out_shape=jax.ShapeDtypeStruct((rows, width), jnp.bfloat16),
        scratch_shapes=[pltpu.SemaphoreType.DMA((len(pieces),))],
        compiler_params=pltpu.CompilerParams(vmem_limit_bytes=SMALL),
        name="unpack",
    )(place, *pieces)


def attend_kernel(scale, offsets, carried, final, spread, first, bias_ref, place_ref, q_ref, *refs):
    count = len(offsets)
    kv_refs, refs = refs[:count], refs[count:]
    s_ref, o_ref, refs = refs[-2], refs[-1], refs[:-2]
    rows = q_ref.shape[1]
    frame_rows = TPS * rows
    if carried:
        accum_ref, stats_ref = refs[:2]
        refs = refs[2:]
    for h in range(kv_refs[0].shape[-1] // HEAD):
        at = slice(h * HEAD, (h + 1) * HEAD)
        q_at = slice((first + h) * HEAD, (first + h + 1) * HEAD)
        q = q_ref[:, :, q_at].reshape(frame_rows, HEAD)
        tops = [None] * TPS
        for i, offset in enumerate(offsets):
            e = offset + REACH
            k = kv_refs[i][:, 0, :, at].reshape(frame_rows, HEAD)
            s = lax.dot_general(
                k, q, (((1,), (1,)), ((), ())), preferred_element_type=jnp.float32
            )
            for b in range(TPS):
                for a in range(TPS):
                    block = s[b * rows : (b + 1) * rows, a * rows : (a + 1) * rows]
                    block = block + bias_ref[a * SPAN * TPS + e * TPS + b]
                    s_ref[0, i * TPS + b, :, a * rows : (a + 1) * rows] = block
                    top = jnp.max(block, axis=0, keepdims=True)
                    tops[a] = top if tops[a] is None else jnp.maximum(tops[a], top)
        top = jnp.concatenate(tops, axis=1) * scale
        if carried:
            before = stats_ref[h, 0:1]
            top = jnp.maximum(top, before)
            factor = jnp.exp2(before - top)
            total = stats_ref[h, 1:2] * factor
            accum = accum_ref[h] * factor
        else:
            total = jnp.zeros((1, frame_rows), jnp.float32)
            accum = None
        for i in range(count):
            s = s_ref[0, i * TPS : (i + 1) * TPS].reshape(frame_rows, frame_rows)
            w = jnp.exp2(s * scale - top)
            total = total + jnp.sum(w, axis=0, keepdims=True)
            v = kv_refs[i][:, 1, :, at].reshape(frame_rows, HEAD)
            part = lax.dot_general(
                v,
                w.astype(jnp.bfloat16),
                (((0,), (0,)), ((), ())),
                preferred_element_type=jnp.float32,
            )
            accum = part if accum is None else accum + part
        if final:
            out = (accum / total).T.reshape(TPS, rows, HEAD).astype(jnp.bfloat16)
            if spread:
                o_ref[h % 2] = out
                for t in range(TPS):
                    refs[t][:, at] = o_ref[h % 2, place_ref[0] ^ t]
            else:
                refs[0][:, :, at] = out
        else:
            refs[0][h] = accum
            refs[1][h, 0:1] = top
            refs[1][h, 1:2] = total


def attend(bias, place, q, kvs, first, carry=None, final=True, spread=False):
    offsets = sorted(kvs)
    groups, _, rows, cols = kvs[offsets[0]].shape
    heads = cols // HEAD
    queries = groups * rows
    keys = len(offsets) * queries
    if spread:
        out_shape = [jax.ShapeDtypeStruct((rows, cols), jnp.bfloat16)] * groups
    elif final:
        out_shape = jax.ShapeDtypeStruct((groups, rows, cols), jnp.bfloat16)
    else:
        out_shape = [
            jax.ShapeDtypeStruct((heads, HEAD, queries), jnp.float32),
            jax.ShapeDtypeStruct((heads, 2, queries), jnp.float32),
        ]
    whole = pl.BlockSpec(memory_space=pltpu.VMEM)
    arrays = [q] + [kvs[o] for o in offsets] + list(carry or ())
    return pl.pallas_call(
        functools.partial(
            attend_kernel,
            math.log2(math.e) / math.sqrt(HEAD),
            offsets,
            carry is not None,
            final,
            spread,
            first,
        ),
        in_specs=[pl.BlockSpec(memory_space=pltpu.SMEM)] * 2 + [whole] * len(arrays),
        out_shape=out_shape,
        out_specs=jax.tree.map(lambda _: whole, out_shape),
        scratch_shapes=[
            pltpu.VMEM((1, len(offsets) * TPS, rows, queries), jnp.float32),
            pltpu.VMEM((2, TPS, rows, HEAD), jnp.bfloat16),
        ],
        compiler_params=pltpu.CompilerParams(
            vmem_limit_bytes=(6 + 2 * len(offsets)) * 1024 * 1024
        ),
        cost_estimate=pl.CostEstimate(
            flops=4 * heads * queries * keys * HEAD,
            bytes_accessed=2 * cols * (2 * queries + 2 * keys),
            transcendentals=heads * queries * keys,
        ),
        name="attend",
    )(bias, place, *arrays)


def tile_bias(tile_order, tile_mask, position, frames):
    pad = REACH * TPS
    padded = jnp.pad(tile_order, (pad, pad))
    near = lax.dynamic_slice_in_dim(padded, position * TPS, SPAN * TPS).reshape(SPAN, TPS)
    near_frames = position + jnp.arange(-REACH, REACH + 1, dtype=jnp.int32)[:, None]
    inside = (near_frames >= 0) & (near_frames < frames)
    spatial = near - near_frames * TPS
    spatial = jnp.where(near_frames >= frames // 2, traded(spatial), spatial)
    own = lax.dynamic_slice_in_dim(tile_order, position * TPS, TPS) - position * TPS
    own = jnp.where(position >= frames // 2, traded(own), own)
    rows = lax.dynamic_slice_in_dim(tile_mask, position * TPS, TPS, 0).reshape(TPS, SPAN, TPS)
    ids = jnp.arange(TPS, dtype=jnp.int32)
    pick_q = own[:, None] == ids
    pick_k = (spatial[:, :, None] == ids) & inside[:, :, None]
    hit = (
        pick_q[:, None, None, :, None]
        & pick_k[None, :, :, None, :]
        & (rows != 0).transpose(1, 0, 2)[None, :, None, :, :]
    )
    allowed = jnp.any(hit, axis=(3, 4))
    return jnp.where(allowed, 0.0, NEG).astype(jnp.float32).reshape(-1)


def partner(u, frame, frames):
    return u ^ 2 if frame >= frames // 2 and u % 2 else u


def traded(slots):
    return jnp.stack([slots[..., i ^ 2 if i % 2 else i] for i in range(TPS)], axis=-1)


def shifted(block, distance, frames, groups):
    route = []
    for i in range(frames):
        j = i + distance
        if 0 <= j < frames:
            for u in range(groups):
                to = partner(partner(u, i, frames), j, frames)
                route.append((i * groups + u, j * groups + to))
    return lax.ppermute(block, AXES, route)


def exchanged(x, frames, groups):
    places = [
        [f * groups + partner(p, f, frames) for p in range(groups)] for f in range(frames)
    ]
    return lax.all_to_all(
        x, AXES, split_axis=0, concat_axis=0, axis_index_groups=places, tiled=True
    )


def swapped(x, step, frames, groups):
    route = []
    for f in range(frames):
        for u in range(groups):
            to = partner(partner(u, f, frames) ^ step, f, frames)
            route.append((f * groups + u, f * groups + to))
    return lax.ppermute(x, AXES, route)


def after(x, *others):
    return lax.optimization_barrier((x, *others))[0]


def per_device(queries, keys, values, tile_order, tile_mask):
    groups = lax.axis_size("uly")
    frames = lax.axis_size("blk")
    position = lax.axis_index("blk")
    move = functools.partial(shifted, frames=frames, groups=groups)
    def spread_out(parts):
        moved = {t: swapped(parts[t], t, frames, groups) for t in (2, 3, 1)}
        return [parts[0]] + [moved[t] for t in (1, 2, 3)]

    swap = functools.partial(exchanged, frames=frames, groups=groups)
    u = lax.axis_index("uly")
    place = jnp.where((position >= frames // 2) & (u % 2 == 1), u ^ 2, u).astype(jnp.int32).reshape(1)
    kv0 = pack_kv(keys, values, groups, CHUNKS[0], 0)
    kv1 = pack_kv(keys, values, groups, CHUNKS[1], CHUNKS[0])
    q = pack_q(queries, groups)
    bias = tile_bias(tile_order, tile_mask, position, frames)

    own0 = swap(kv0)
    up0, down0 = move(own0, 1), move(own0, -1)
    own1 = swap(after(kv1, own0))
    own_q = swap(after(q, own1))
    up1, down1 = move(own1, 1), move(own1, -1)
    up0b, down0b = move(up0, 1), move(down0, -1)
    up1b, down1b = move(up1, 1), move(down1, -1)
    part1 = attend(bias, place, own_q, {-1: up1, 0: own1, 1: down1}, CHUNKS[0], None, False)
    bias0 = after(bias, part1[0])
    part0 = attend(bias0, place, own_q, {-1: up0, 0: own0, 1: down0}, 0, None, False)
    part0 = attend(after(bias0, part0[0]), place, own_q, {-2: up0b}, 0, part0, False)
    out0 = attend(after(bias0, part0[0]), place, own_q, {2: down0b}, 0, part0, spread=True)
    res0 = spread_out(out0)
    bias1 = after(bias, out0[0])
    part1 = attend(bias1, place, own_q, {-2: up1b}, CHUNKS[0], part1, False)
    bias1 = after(bias1, part1[0])
    out1 = attend(bias1, place, own_q, {2: down1b}, CHUNKS[0], part1, spread=True)
    return unpack(place, [res0, spread_out(out1)])


def solution(mesh):
    return jax.shard_map(
        per_device,
        mesh=mesh,
        in_specs=(
            P(AXES, None),
            P(AXES, None),
            P(AXES, None),
            P(),
            P(),
        ),
        out_specs=P(AXES, None),
        check_vma=False,
    )
```
